256 devices in a mesh: gx: 32 (over y, z_hi, x), gy: 8 (over z_lo, core).
Axes of the slice: x: 4, y: 4, z: 8 (z_hi: 2, z_lo: 4; z = z_hi * 4 + z_lo), core: 2. Of those that a mesh axis runs over, the one named last changes fastest.
Arguments:
- species_field: float32 [256, 1024, 1024], P(None, 'gx', 'gy'), may hold values from -6 to 6
- basis_one: float32 [1024, 256], replicated, may hold values from -0.1875 to 0.1875
- basis_two: float32 [1024, 256], replicated, may hold values from -0.1875 to 0.1875
Outputs:
- core_tensor: float32 [256, 256, 256], P('gx', 'gy')
The draws below stay inside these ranges and needn't reach their ends.
All inputs are finite; a program needn't handle non-finite values.
Results may differ from the reference program's by a relative error of at most 0.000084.
Values sent between devices are 32-bit elements; how exact they have to be, the bound alone decides.
No kernel may reach another device: no remote copies, remote signals or barrier semaphores. Data moves between devices by JAX's collectives and lax.ppermute only.
A program may use at most 128 MiB of HBM per device.

```python
import jax
import jax.numpy as jnp
from jax import lax

DEPTH = 256
RANK = 256
N1 = 1024
N2 = 1024


def raised(result, stream_key, source, target, blocks, factor):
    def block_of(axis_at):
        return (jnp.arange(result.shape[axis_at]) // (result.shape[axis_at] // blocks)).reshape((-1,) + (1,) * (result.ndim - 1 - axis_at))

    first = jax.random.permutation(stream_key, blocks)[block_of(target)]
    far = (block_of(target) + blocks // 2) % blocks
    return jnp.where((block_of(source) == first) | (block_of(source) == far), factor * result, result)


def block_scale(key, shape, shards, least, high):
    gain, own = 1.0, jax.random.fold_in(key, 6)
    for axis_at, shards_of in shards:
        steps = jnp.exp(jax.random.uniform(jax.random.fold_in(own, axis_at), (shards_of,), jnp.float32, least / len(shards), high / len(shards)))
        gain = gain * jnp.repeat(steps, shape[axis_at] // shards_of).reshape([-1 if axis == axis_at else 1 for axis in range(len(shape))])
    return gain


def gaussian(rng, shape, spread, bound, split=(), kind=jnp.bfloat16):
    factor_of = block_scale(rng, shape, split, -0.22, 0.18) if split else 1.0
    drawn = jax.random.normal(rng, shape, jnp.float32) * spread * factor_of
    return jnp.minimum(jnp.maximum(drawn, -bound), bound).astype(kind)


def gaussian_with(key, dims, deviation, reach, cuts, heavy, kind=jnp.bfloat16):
    array = deviation * jax.random.normal(key, dims, jnp.float32)
    if cuts:
        array = array * block_scale(key, dims, cuts, -0.22, 0.18)
    return jnp.clip(raised(array, jax.random.fold_in(key, 3), *heavy), -reach, reach).astype(kind)


def setup_inputs(seed: int = 0) -> dict:
    key_list = jax.random.split(jax.random.key(seed), 4)
    species_field = gaussian_with(key_list[0], (DEPTH, N1, N2), 1.0, 6.0, ((1, 32), (2, 8)), (1, 0, 32, 2.75), jnp.float32)
    basis_one = gaussian(key_list[1], (N1, RANK), N1 ** -0.5, 0.1875, (), jnp.float32)
    basis_two = gaussian(key_list[2], (N2, RANK), N2 ** -0.5, 0.1875, (), jnp.float32)
    return dict(species_field=species_field, basis_one=basis_one, basis_two=basis_two)


def reference(species_field, basis_one, basis_two):
    def per_depth(plane):
        reduced = jnp.dot(basis_one.T, plane, precision=lax.Precision.HIGHEST)
        return jnp.dot(reduced, basis_two, precision=lax.Precision.HIGHEST)

    return lax.map(per_depth, species_field)
```

```python
import functools

import jax
import jax.numpy as jnp
from jax import lax
from jax.experimental import pallas as pl
from jax.experimental.pallas import tpu as pltpu
from jax.sharding import Mesh, PartitionSpec as P

AXES = ("y", "zh", "x", "zl", "c")
SIZES = (4, 2, 4, 4, 2)
CHUNKS = (2, 2)


def permuted(value, dz, flip):
    pairs = []
    for y in range(4):
        for z in range(8):
            for x in range(4):
                for c in range(2):
                    def at(z, c):
                        return (((y * 2 + z // 4) * 4 + x) * 4 + z % 4) * 2 + c
                    pairs.append((at(z, c), at((z + dz) % 8, c ^ flip)))
    return lax.ppermute(value, AXES, pairs)


def halves(value):
    high = lax.reduce_precision(value, 8, 7)
    return high.astype(jnp.bfloat16), (value - high).astype(jnp.bfloat16)


def dot3(left, right):
    dot = functools.partial(jnp.dot, preferred_element_type=jnp.float32)
    return dot(left[0], right[0]) + (dot(left[0], right[1]) + dot(left[1], right[0]))


def split(value):
    high = value.astype(jnp.bfloat16)
    return high, (value - high.astype(jnp.float32)).astype(jnp.bfloat16)


def contract_kernel(z_ref, x_ref, one_h, one_l, two_h, two_l, out_ref):
    block = jnp.concatenate([x_ref[:, c, 0, 0].reshape(512, 128) for c in range(2)], axis=1)
    reduced = dot3((one_h[...], one_l[...]), split(block))
    partial = dot3(split(reduced), (two_h[...], two_l[...]))
    zh, k = pl.program_id(0), pl.program_id(1)
    for zl in range(4):
        away = (zh * 4 + zl + 8 - z_ref[0]) % 8
        out_ref[away, k] = partial[zl * 64:(zl + 1) * 64]


def contract(position, received, one, two):
    n = received.shape[3]
    whole = lambda shape: pl.BlockSpec(shape, lambda zh, k, z: (0,) * len(shape))
    return pl.pallas_call(
        contract_kernel,
        grid_spec=pltpu.PrefetchScalarGridSpec(
            num_scalar_prefetch=1,
            grid=(2, n),
            in_specs=[pl.BlockSpec((16, 2, 1, 1, 32, 128), lambda zh, k, z: (0, 0, zh, k, 0, 0))]
            + [whole((256, 512))] * 2 + [whole((256, 256))] * 2,
            out_specs=whole((8, n, 64, 256)),
        ),
        out_shape=jax.ShapeDtypeStruct((8, n, 64, 256), jnp.float32),
        compiler_params=pltpu.CompilerParams(vmem_limit_bytes=24 << 20),
        cost_estimate=pl.CostEstimate(flops=n * 2 * 3 * 2 * 256 * 256 * 768, bytes_accessed=n * (3 << 20) // 2, transcendentals=0),
    )(position, received, *one, *two)


def scattered(parts, c):
    half = lambda v, which: lax.dynamic_slice_in_dim(v, which * 32, 32, 1)
    up = permuted(parts[4, :, :32], 1, 0)
    down = permuted(parts[4, :, 32:], -1, 0)
    swapped = permuted(half(parts[0], 1 - c), 0, 1)
    up = jnp.concatenate([parts[3, :, :32] + up, parts[3, :, 32:]], axis=1)
    down = jnp.concatenate([parts[5, :, :32], parts[5, :, 32:] + down], axis=1)
    up, down = permuted(up, 1, 0) + parts[2], permuted(down, -1, 0) + parts[6]
    up, down = permuted(up, 1, 0) + parts[1], permuted(down, -1, 0) + parts[7]
    own = half(parts[0], c) + permuted(half(up, c), 1, 0) + permuted(half(down, c), -1, 0)
    other = swapped + permuted(half(up, 1 - c), 1, 1) + permuted(half(down, 1 - c), -1, 1)
    return jnp.stack([jnp.where(c == 0, own, other), jnp.where(c == 0, other, own)])


def on_device(species_field, basis_one, basis_two):
    zh, zl, c = lax.axis_index("zh"), lax.axis_index("zl"), lax.axis_index("c")
    position = (zh * 4 + zl).astype(jnp.int32).reshape(1)
    rows = lax.dynamic_index_in_dim(basis_one.reshape(4, 2, 4, 32, 256), zh, 1, keepdims=False)
    one = halves(rows.reshape(512, 256).T)
    two = halves(lax.dynamic_slice_in_dim(basis_two, zl * 256, 256, 0))
    field = species_field.reshape(4, 2, 4, 2, 4, 32, 128)
    outs, start = [], 0
    for n in CHUNKS:
        piece = field[:, :, :, :, start:start + n].transpose(0, 2, 3, 1, 4, 5, 6).reshape(32 * 2 * n, 32, 128)
        moved = lax.all_to_all(piece, ("y", "x", "c"), split_axis=0, concat_axis=0, tiled=True)
        parts = contract(position, moved.reshape(16, 2, 2, n, 32, 128), one, two)
        outs.append(scattered(parts, c))
        start += n
    return jnp.concatenate(outs, axis=1).reshape(8, 32, 256)


def solution(mesh):
    fine = Mesh(mesh.devices.reshape(SIZES), AXES)
    placed = (P(None, ("y", "zh", "x"), ("zl", "c")), P(), P())
    return jax.shard_map(
        on_device, mesh=fine, in_specs=placed, out_specs=P(("y", "zh", "x"), ("zl", "c"), None), check_vma=False
    )
```

```python
import functools

import jax
import jax.numpy as jnp
from jax import lax
from jax.experimental import pallas as pl
from jax.experimental.pallas import tpu as pltpu
from jax.sharding import Mesh, PartitionSpec as P

AXES = ("y", "zh", "x", "zl", "c")
SIZES = (4, 2, 4, 4, 2)
PLANE = ("y", "x", "c")
VMEM = pl.BlockSpec(memory_space=pltpu.VMEM)
SMEM = pl.BlockSpec(memory_space=pltpu.SMEM)
ANY = pl.BlockSpec(memory_space=pl.ANY)
f32 = functools.partial(jax.ShapeDtypeStruct, dtype=jnp.float32)
dot = functools.partial(jnp.dot, preferred_element_type=jnp.float32)
params = functools.partial(pltpu.CompilerParams, vmem_limit_bytes=20 << 20)


def along(value, dz, flip=0):
    pairs = []
    for y in range(4):
        for z in range(8):
            for x in range(4):
                for c in range(2):

                    def at(z, c):
                        return (((y * 2 + z // 4) * 4 + x) * 4 + z % 4) * 2 + c

                    pairs.append((at(z, c), at((z + dz) % 8, c ^ flip)))
    return lax.ppermute(value, AXES, pairs)


def split(value):
    high = value.astype(jnp.bfloat16)
    return high, (value - high.astype(jnp.float32)).astype(jnp.bfloat16)


def pack_kernel(field_ref, packed_ref, sems):
    copies = []
    for zh in range(2):
        for c in range(2):
            copies.append(pltpu.make_async_copy(field_ref.at[:, zh, :, c], packed_ref.at[:, :, c, zh], sems.at[2 * zh + c]))
    for copy in copies:
        copy.start()
    for copy in copies:
        copy.wait()


def pack(field):
    return pl.pallas_call(
        pack_kernel,
        in_specs=[ANY],
        out_specs=VMEM,
        out_shape=f32((4, 4, 2, 2, 4, 32, 128)),
        scratch_shapes=[pltpu.SemaphoreType.DMA((4,))],
        compiler_params=params(),
    )(field)


def prepare_kernel(one_ref, two_ref, one_out, two_out):
    for zh in range(2):
        high, low = split(one_ref[:, zh].reshape(512, 256).T)
        one_out[zh] = jnp.concatenate([high, high, low], axis=1)
    for zl in range(4):
        high, low = split(two_ref[256 * zl:256 * zl + 256])
        two_out[zl] = jnp.concatenate([high, high, low], axis=0)


def prepare(basis_one, basis_two):
    return pl.pallas_call(
        prepare_kernel,
        in_specs=[VMEM] * 2,
        out_specs=[VMEM] * 2,
        out_shape=[jax.ShapeDtypeStruct((2, 256, 1536), jnp.bfloat16), jax.ShapeDtypeStruct((4, 768, 256), jnp.bfloat16)],
        compiler_params=params(),
        cost_estimate=pl.CostEstimate(flops=1 << 26, bytes_accessed=5 << 20, transcendentals=0),
    )(basis_one.reshape(4, 2, 4, 32, 256), basis_two)


def first_kernel(at_ref, x_ref, one_ref, two_ref, out_ref, reduced_ref):
    z, core = at_ref[0], at_ref[1]
    one, two = one_ref[z // 4], two_ref[z % 4]
    for t in range(8):
        block = jnp.concatenate([x_ref[:, c, t // 4, t % 4].reshape(512, 128) for c in range(2)], axis=1)
        high, low = split(block)
        high, low = split(dot(one, jnp.concatenate([high, low, high], axis=0)))
        reduced_ref[t] = jnp.concatenate([high, low, high], axis=1)
    partial = dot(reduced_ref[...].reshape(2048, 768), two).reshape(8, 256, 256)
    for t in range(8):
        for b in range(8):
            away = (t // 4 * 4 + b // 2 + 8 - z) % 8
            out_ref[away, (b % 2) ^ core, t % 4] = partial[t, 32 * b:32 * b + 32]


def first_contract(at, received, one, two):
    return pl.pallas_call(
        first_kernel,
        in_specs=[SMEM, VMEM, VMEM, VMEM],
        out_specs=VMEM,
        out_shape=f32((8, 2, 4, 32, 256)),
        scratch_shapes=[pltpu.VMEM((8, 256, 768), jnp.bfloat16)],
        compiler_params=params(),
        cost_estimate=pl.CostEstimate(flops=8 * 3 * 2 * 256 * 256 * 768, bytes_accessed=6 << 20, transcendentals=0),
    )(at, received, one, two)


def finish_kernel(at_ref, first_ref, up_ref, down_ref, swapped_ref, up_cross_ref, down_cross_ref, out_ref):
    core = at_ref[1]
    out_ref[pl.ds(4 * core, 4)] = first_ref[...] + (up_ref[...] + down_ref[...])
    out_ref[pl.ds(4 - 4 * core, 4)] = swapped_ref[...] + (up_cross_ref[...] + down_cross_ref[...])


def finish(at, *pieces):
    return pl.pallas_call(
        finish_kernel,
        in_specs=[SMEM] + [VMEM] * 6,
        out_specs=VMEM,
        out_shape=f32((8, 32, 256)),
        compiler_params=params(),
    )(at, *pieces)


def on_device(species_field, basis_one, basis_two):
    zh, zl, c = lax.axis_index("zh"), lax.axis_index("zl"), lax.axis_index("c")
    z = zh * 4 + zl
    at = jnp.stack([z, c]).astype(jnp.int32)
    packed = pack(species_field.reshape(4, 2, 4, 2, 4, 32, 128)).reshape(256, 32, 128)
    packed, at, one, two = lax.optimization_barrier((packed, at, *prepare(basis_one, basis_two)))
    moved = lax.all_to_all(packed, PLANE, split_axis=0, concat_axis=0, tiled=True)
    parts = first_contract(at, moved.reshape(16, 2, 2, 4, 32, 128), one, two)
    up, down = along(parts[4, 0], 1), along(parts[4, 1], -1)
    swapped = along(parts[0, 1], 0, 1)
    up = jnp.stack([parts[3, 0] + up, parts[3, 1]])
    down = jnp.stack([parts[5, 0], parts[5, 1] + down])
    up, down = along(up, 1) + parts[2], along(down, -1) + parts[6]
    up, down = along(up, 1) + parts[1], along(down, -1) + parts[7]
    ends = [along(up[0], 1), along(down[0], -1), swapped, along(up[1], 1, 1), along(down[1], -1, 1)]

    return finish(at, parts[0, 0], *ends)


def solution(mesh):
    fine = Mesh(mesh.devices.reshape(SIZES), AXES)
    placed = (P(None, ("y", "zh", "x"), ("zl", "c")), P(), P())
    return jax.shard_map(
        on_device, mesh=fine, in_specs=placed, out_specs=P(("y", "zh", "x"), ("zl", "c"), None), check_vma=False
    )
```

```python
import functools

import jax
import jax.numpy as jnp
from jax import lax
from jax.experimental import pallas as pl
from jax.experimental.pallas import tpu as pltpu
from jax.sharding import Mesh, PartitionSpec as P

AXES = ("y", "zh", "x", "zp", "zn", "c")
SIZES = (4, 2, 4, 2, 2, 2)
VMEM = pl.BlockSpec(memory_space=pltpu.VMEM)
f32 = functools.partial(jax.ShapeDtypeStruct, dtype=jnp.float32)
dot = functools.partial(jnp.dot, preferred_element_type=jnp.float32)
params = functools.partial(pltpu.CompilerParams, vmem_limit_bytes=24 << 20)


def split(value):
    high = value.astype(jnp.bfloat16)
    return high, (value - high.astype(jnp.float32)).astype(jnp.bfloat16)


def pack_kernel(at_ref, field_ref, packed_ref, sems):
    del at_ref
    copies = [
        pltpu.make_async_copy(field_ref.at[:, zh, :, q], packed_ref.at[:, :, q, zh], sems.at[4 * zh + q])
        for zh in range(2)
        for q in range(4)
    ]
    for copy in copies:
        copy.start()
    for copy in copies:
        copy.wait()


def pack(at, field):
    return pl.pallas_call(
        pack_kernel,
        in_specs=[pl.BlockSpec(memory_space=pltpu.SMEM), pl.BlockSpec(memory_space=pl.ANY)],
        out_specs=VMEM,
        out_shape=f32((4, 4, 4, 2, 2, 32, 128)),
        scratch_shapes=[pltpu.SemaphoreType.DMA((8,))],
        compiler_params=params(),
    )(at, field)


def contract_kernel(at_ref, x_ref, one_ref, two_ref, out_ref, reduced_ref):
    z = at_ref[0]
    high, low = split(one_ref[:, z // 4].reshape(512, 256).T)
    one = jnp.concatenate([high, high, low], axis=1)
    for t in range(4):
        block = jnp.concatenate([x_ref[:, q, t // 2, t % 2].reshape(512, 128) for q in range(4)], axis=1)
        high, low = split(block)
        high, low = split(dot(one, jnp.concatenate([high, low, high], axis=0)))
        reduced_ref[t] = jnp.concatenate([high, low, high], axis=1)
    high, low = split(two_ref[pl.ds(pl.multiple_of(z // 2 % 2 * 512, 512), 512)])
    partial = dot(reduced_ref[...].reshape(1024, 1536), jnp.concatenate([high, high, low], axis=0)).reshape(4, 256, 256)
    for t in range(4):
        for b in range(8):
            out_ref[t // 2 * 8 + b, t % 2] = partial[t, 32 * b:32 * b + 32]


def contract(at, received, basis_one, basis_two):
    return pl.pallas_call(
        contract_kernel,
        in_specs=[pl.BlockSpec(memory_space=pltpu.SMEM)] + [VMEM] * 3,
        out_specs=VMEM,
        out_shape=f32((16, 2, 32, 256)),
        scratch_shapes=[pltpu.VMEM((4, 256, 1536), jnp.bfloat16)],
        compiler_params=params(),
        cost_estimate=pl.CostEstimate(flops=4 * 3 * 2 * 256 * 256 * 1536, bytes_accessed=6 << 20, transcendentals=0),
    )(at, received, basis_one.reshape(4, 2, 4, 32, 256), basis_two)


def finish_kernel(part_ref, out_ref):
    for q in range(4):
        terms = [part_ref[zh, zp, q] for zh in range(2) for zp in range(2)]
        out_ref[2 * q:2 * q + 2] = (terms[0] + terms[1]) + (terms[2] + terms[3])


def finish(parts):
    return pl.pallas_call(
        finish_kernel, in_specs=[VMEM], out_specs=VMEM, out_shape=f32((8, 32, 256)), compiler_params=params()
    )(parts)


def on_device(species_field, basis_one, basis_two):
    z = lax.axis_index("zh") * 4 + lax.axis_index("zp") * 2
    at = z.astype(jnp.int32).reshape(1)
    packed = pack(at, species_field.reshape(4, 2, 4, 4, 2, 32, 128))
    moved = lax.all_to_all(packed.reshape(256, 32, 128), ("y", "x", "zn", "c"), split_axis=0, concat_axis=0, tiled=True)
    parts = contract(at, moved.reshape(16, 4, 2, 2, 32, 128), basis_one, basis_two)
    parts = lax.all_to_all(parts, ("zh", "zp", "zn", "c"), split_axis=0, concat_axis=0, tiled=True)
    return finish(parts.reshape(2, 2, 4, 2, 32, 256))


def solution(mesh):
    fine = Mesh(mesh.devices.reshape(SIZES), AXES)
    placed = (P(None, ("y", "zh", "x"), ("zp", "zn", "c")), P(), P())
    return jax.shard_map(
        on_device, mesh=fine, in_specs=placed, out_specs=P(("y", "zh", "x"), ("zp", "zn", "c"), None), check_vma=False
    )
```

```python
import functools

import jax
import jax.numpy as jnp
from jax import lax
from jax.experimental import pallas as pl
from jax.experimental.pallas import tpu as pltpu
from jax.sharding import Mesh, PartitionSpec as P

AXES = ("y", "zh", "x", "zp", "zn", "c")
SIZES = (4, 2, 4, 2, 2, 2)
DISTANCES = (-2, 2, -3, 3, 4, -1, 1)
VMEM = pl.BlockSpec(memory_space=pltpu.VMEM)
SMEM = pl.BlockSpec(memory_space=pltpu.SMEM)
f32 = functools.partial(jax.ShapeDtypeStruct, dtype=jnp.float32)
dot = functools.partial(jnp.dot, preferred_element_type=jnp.float32)
params = functools.partial(pltpu.CompilerParams, vmem_limit_bytes=24 << 20)


def along(value, distance):
    pairs = []
    for y in range(4):
        for z in range(8):
            for x in range(4):
                for c in range(2):

                    def at(z):
                        return (((y * 2 + z // 4) * 4 + x) * 4 + z % 4) * 2 + c

                    pairs.append((at(z), at((z + distance) % 8)))
    return lax.ppermute(value, AXES, pairs)


def split(value):
    high = value.astype(jnp.bfloat16)
    return high, (value - high.astype(jnp.float32)).astype(jnp.bfloat16)


def pack_kernel(z_ref, core_ref, field_ref, packed_ref, sems):
    del z_ref, core_ref
    copies = [
        pltpu.make_async_copy(field_ref.at[:, zh, :, q], packed_ref.at[:, :, q, zh], sems.at[4 * zh + q])
        for zh in range(2)
        for q in range(4)
    ]
    for copy in copies:
        copy.start()
    for copy in copies:
        copy.wait()


def pack(z, core, field):
    return pl.pallas_call(
        pack_kernel,
        in_specs=[SMEM, SMEM, pl.BlockSpec(memory_space=pl.ANY)],
        out_specs=VMEM,
        out_shape=f32((4, 4, 4, 2, 2, 32, 128)),
        scratch_shapes=[pltpu.SemaphoreType.DMA((8,))],
        compiler_params=params(),
    )(z, core, field)


def contract_kernel(z_ref, core_ref, x_ref, one_ref, two_ref, out_ref, reduced_ref):
    z, core = z_ref[0], core_ref[0]
    high, low = split(one_ref[:, z // 4].reshape(512, 256).T)
    one = jnp.concatenate([high, high, low], axis=1)
    for t in range(4):
        block = jnp.concatenate([x_ref[:, q, t // 2, t % 2].reshape(512, 128) for q in range(4)], axis=1)
        high, low = split(block)
        high, low = split(dot(one, jnp.concatenate([high, low, high], axis=0)))
        reduced_ref[t] = jnp.concatenate([high, low, high], axis=1)
    high, low = split(two_ref[pl.ds(pl.multiple_of(z // 2 % 2 * 512, 512), 512)])
    partial = dot(reduced_ref[...].reshape(1024, 1536), jnp.concatenate([high, high, low], axis=0)).reshape(4, 256, 256)
    for t in range(4):
        for b in range(8):
            away = (4 * (t // 2) + b // 2 + 8 - z) % 8
            out_ref[away, (b % 2) ^ core, t % 2] = partial[t, 32 * b:32 * b + 32]


def contract(z, core, received, basis_one, basis_two):
    return pl.pallas_call(
        contract_kernel,
        in_specs=[SMEM] * 2 + [VMEM] * 3,
        out_specs=VMEM,
        out_shape=f32((8, 2, 2, 32, 256)),
        scratch_shapes=[pltpu.VMEM((4, 256, 1536), jnp.bfloat16)],
        compiler_params=params(),
        cost_estimate=pl.CostEstimate(flops=4 * 3 * 2 * 256 * 256 * 1536, bytes_accessed=6 << 20, transcendentals=0),
    )(z, core, received, basis_one.reshape(4, 2, 4, 32, 256), basis_two)


def add_kernel(first_ref, *refs):
    parts, (own_ref, other_ref) = dict(zip(DISTANCES, refs)), refs[7:]
    for core, out_ref in enumerate((own_ref, other_ref)):
        for odd in range(2):
            terms = [parts[d][core] for d in DISTANCES if d % 2 == odd]
            if not odd:
                terms.append(first_ref[0, core])
            out_ref[odd] = (terms[0] + terms[1]) + (terms[2] + terms[3])


def add(parts, received):
    return pl.pallas_call(
        add_kernel, in_specs=[VMEM] * 8, out_specs=[VMEM] * 2, out_shape=[f32((2, 2, 32, 256))] * 2, compiler_params=params()
    )(parts, *received)


def finish_kernel(z_ref, core_ref, own_ref, swapped_ref, out_ref):
    zn, core = z_ref[0] % 2, core_ref[0]
    for odd in range(2):
        out_ref[pl.ds(4 * (zn ^ odd) + 2 * core, 2)] = own_ref[odd]
        out_ref[pl.ds(4 * (zn ^ odd) + 2 - 2 * core, 2)] = swapped_ref[odd]


def finish(z, core, own, swapped):
    return pl.pallas_call(
        finish_kernel, in_specs=[SMEM] * 2 + [VMEM] * 2, out_specs=VMEM, out_shape=f32((8, 32, 256)), compiler_params=params()
    )(z, core, own, swapped)


def on_device(species_field, basis_one, basis_two):
    z = sum(lax.axis_index(axis) * size for axis, size in (("zh", 4), ("zp", 2), ("zn", 1))).astype(jnp.int32).reshape(1)
    core = lax.axis_index("c").astype(jnp.int32).reshape(1)
    packed = pack(z, core, species_field.reshape(4, 2, 4, 4, 2, 32, 128))
    moved = lax.all_to_all(packed.reshape(256, 32, 128), ("y", "x", "zn", "c"), split_axis=0, concat_axis=0, tiled=True)
    parts = contract(z, core, moved.reshape(16, 4, 2, 2, 32, 128), basis_one, basis_two)
    own, other = add(parts[:1], [along(parts[distance % 8], distance) for distance in DISTANCES])
    return finish(z, core, own, lax.ppermute(other, "c", [(0, 1), (1, 0)]))


def solution(mesh):
    fine = Mesh(mesh.devices.reshape(SIZES), AXES)
    placed = (P(None, ("y", "zh", "x"), ("zp", "zn", "c")), P(), P())
    return jax.shard_map(
        on_device, mesh=fine, in_specs=placed, out_specs=P(("y", "zh", "x"), ("zp", "zn", "c"), None), check_vma=False
    )
```

```python
import functools

import jax
import jax.numpy as jnp
from jax import lax
from jax.experimental import pallas as pl
from jax.experimental.pallas import tpu as pltpu
from jax.sharding import Mesh, PartitionSpec as P

AXES = ("y", "zh", "x", "zp", "zn", "c")
SIZES = (4, 2, 4, 2, 2, 2)
FIRST = (1, 2, 4, 7)
SENDS = ((1, 2, 3, 0), (0, 3, 2, 1), (2, 1, 0, 3), (3, 0, 1, 2))
TARGETS = [dict(zip(FIRST, to)) | {7 - z: 7 - t for z, t in zip(FIRST, to)} for to in SENDS]
ORDER = (1, 3, 2, 0)
VMEM = pl.BlockSpec(memory_space=pltpu.VMEM)
SMEM = pl.BlockSpec(memory_space=pltpu.SMEM)
f32 = functools.partial(jax.ShapeDtypeStruct, dtype=jnp.float32)
dot = functools.partial(jnp.dot, preferred_element_type=jnp.float32)
params = functools.partial(pltpu.CompilerParams, vmem_limit_bytes=24 << 20)


def send(value, number):
    pairs = []
    for y in range(4):
        for z in range(8):
            for x in range(4):
                for c in range(2):

                    def at(z):
                        return (((y * 2 + z // 4) * 4 + x) * 4 + z % 4) * 2 + c

                    pairs.append((at(z), at(TARGETS[number][z])))
    return lax.ppermute(value, AXES, pairs)


def split(value):
    high = value.astype(jnp.bfloat16)
    return high, (value - high.astype(jnp.float32)).astype(jnp.bfloat16)


def pack_kernel(z_ref, core_ref, field_ref, packed_ref, sems):
    del core_ref
    first = 1 - (z_ref[0] // 4 ^ z_ref[0] // 2 % 2)
    copies = [
        pltpu.make_async_copy(field_ref.at[:, first ^ zn, :, c], packed_ref.at[:, :, zn, c], sems.at[2 * zn + c])
        for zn in range(2)
        for c in range(2)
    ]
    for copy in copies:
        copy.start()
    for copy in copies:
        copy.wait()


def pack(z, core, field):
    return pl.pallas_call(
        pack_kernel,
        in_specs=[SMEM, SMEM, pl.BlockSpec(memory_space=pl.ANY)],
        out_specs=VMEM,
        out_shape=f32((4, 4, 2, 2, 4, 32, 128)),
        scratch_shapes=[pltpu.SemaphoreType.DMA((4,))],
        compiler_params=params(),
    )(z, core, field)


def contract_kernel(z_ref, core_ref, x_ref, one_ref, two_ref, out_ref, reduced_ref):
    z, core = z_ref[0], core_ref[0]
    high, low = split(one_ref[:, z // 4].reshape(512, 256).T)
    one = jnp.concatenate([high, high, low], axis=1)
    for t in range(4):
        block = jnp.concatenate([x_ref[:, q, t].reshape(512, 128) for q in range(4)], axis=1)
        high, low = split(block)
        high, low = split(dot(one, jnp.concatenate([high, low, high], axis=0)))
        reduced_ref[t] = jnp.concatenate([high, low, high], axis=1)
    high, low = split(two_ref[pl.ds(pl.multiple_of(z // 2 % 2 * 512, 512), 512)])
    partial = dot(reduced_ref[...].reshape(1024, 1536), jnp.concatenate([high, high, low], axis=0)).reshape(4, 256, 256)
    for b in range(8):
        table = sum(n << 2 * chip for n in range(4) for chip, to in TARGETS[n].items() if to % 4 == b // 2)
        number = (table >> 2 * z) & 3
        for t in range(4):
            out_ref[number, (b % 2) ^ core, t] = partial[t, 32 * b:32 * b + 32]


def contract(z, core, received, basis_one, basis_two):
    return pl.pallas_call(
        contract_kernel,
        in_specs=[SMEM] * 2 + [VMEM] * 3,
        out_specs=VMEM,
        out_shape=f32((4, 2, 4, 32, 256)),
        scratch_shapes=[pltpu.VMEM((4, 256, 1536), jnp.bfloat16)],
        compiler_params=params(),
        cost_estimate=pl.CostEstimate(flops=4 * 3 * 2 * 256 * 256 * 1536, bytes_accessed=6 << 20, transcendentals=0),
    )(z, core, received, basis_one.reshape(4, 2, 4, 32, 256), basis_two)


def add_kernel(a_ref, b_ref, c_ref, d_ref, own_ref, other_ref):
    for core, out_ref in enumerate((own_ref, other_ref)):
        out_ref[...] = (a_ref[core] + b_ref[core]) + (c_ref[core] + d_ref[core])


def add(received):
    return pl.pallas_call(
        add_kernel, in_specs=[VMEM] * 4, out_specs=[VMEM] * 2, out_shape=[f32((4, 32, 256))] * 2, compiler_params=params()
    )(*received)


def finish_kernel(core_ref, own_ref, swapped_ref, out_ref):
    core = core_ref[0]
    out_ref[pl.ds(4 * core, 4)] = own_ref[...]
    out_ref[pl.ds(4 - 4 * core, 4)] = swapped_ref[...]


def finish(core, own, swapped):
    return pl.pallas_call(
        finish_kernel, in_specs=[SMEM, VMEM, VMEM], out_specs=VMEM, out_shape=f32((8, 32, 256)), compiler_params=params()
    )(core, own, swapped)


def on_device(species_field, basis_one, basis_two):
    z = sum(lax.axis_index(axis) * size for axis, size in (("zh", 4), ("zp", 2), ("zn", 1))).astype(jnp.int32).reshape(1)
    core = lax.axis_index("c").astype(jnp.int32).reshape(1)
    packed = pack(z, core, species_field.reshape(4, 2, 4, 2, 4, 32, 128))
    moved = lax.all_to_all(packed.reshape(256, 32, 128), ("y", "x", "zn", "c"), split_axis=0, concat_axis=0, tiled=True)
    parts = contract(z, core, moved.reshape(16, 4, 4, 32, 128), basis_one, basis_two)
    own, other = add([send(parts[number], number) for number in ORDER])
    return finish(core, own, lax.ppermute(other, "c", [(0, 1), (1, 0)]))


def solution(mesh):
    fine = Mesh(mesh.devices.reshape(SIZES), AXES)
    placed = (P(None, ("y", "zh", "x"), ("zp", "zn", "c")), P(), P())
    return jax.shard_map(
        on_device, mesh=fine, in_specs=placed, out_specs=P(("y", "zh", "x"), ("zp", "zn", "c"), None), check_vma=False
    )
```

```python
import functools

import jax
import jax.numpy as jnp
from jax import lax
from jax.experimental import pallas as pl
from jax.experimental.pallas import tpu as pltpu
from jax.sharding import Mesh, PartitionSpec as P

AXES = ("y", "zh", "x", "zp", "zn", "c")
SIZES = (4, 2, 4, 2, 2, 2)
FIRST = (1, 2, 4, 7)
SENDS = ((1, 2, 3, 0), (0, 3, 2, 1), (2, 1, 0, 3), (3, 0, 1, 2))
TARGETS = [dict(zip(FIRST, to)) | {7 - z: 7 - t for z, t in zip(FIRST, to)} for to in SENDS]
ORDER = (1, 3, 2, 0)
VMEM = pl.BlockSpec(memory_space=pltpu.VMEM)
SMEM = pl.BlockSpec(memory_space=pltpu.SMEM)
f32 = functools.partial(jax.ShapeDtypeStruct, dtype=jnp.float32)
dot = functools.partial(jnp.dot, preferred_element_type=jnp.float32)
params = functools.partial(pltpu.CompilerParams, vmem_limit_bytes=24 << 20)


def device(y, z, x, c):
    return (((y * 2 + z // 4) * 4 + x) * 4 + z % 4) * 2 + c


def groups():
    halves = [sorted((z, z + 1), key=lambda chip: chip not in FIRST) for z in range(0, 8, 2)]
    return [[device(y, z, x, c) for y in range(4) for z in pair for x in range(4) for c in range(2)] for pair in halves]


def send(value, number):
    pairs = []
    for y in range(4):
        for z in range(8):
            for x in range(4):
                for c in range(2):
                    pairs.append((device(y, z, x, c), device(y, TARGETS[number][z], x, c)))
    return lax.ppermute(value, AXES, pairs)


def split(value):
    high = value.astype(jnp.bfloat16)
    return high, (value - high.astype(jnp.float32)).astype(jnp.bfloat16)


def contract_kernel(z_ref, core_ref, x_ref, one_ref, two_ref, out_ref, reduced_ref):
    z, core = z_ref[0], core_ref[0]
    first = 1 - (z // 4 ^ z // 2 % 2)
    high, low = split(one_ref[:, z // 4].reshape(512, 256).T)
    one = jnp.concatenate([high, high, low], axis=1)
    for t in range(4):
        block = [x_ref[:, first ^ zn, :, c, t].reshape(512, 128) for zn in range(2) for c in range(2)]
        high, low = split(jnp.concatenate(block, axis=1))
        high, low = split(dot(one, jnp.concatenate([high, low, high], axis=0)))
        reduced_ref[t] = jnp.concatenate([high, low, high], axis=1)
    high, low = split(two_ref[pl.ds(pl.multiple_of(z // 2 % 2 * 512, 512), 512)])
    partial = dot(reduced_ref[...].reshape(1024, 1536), jnp.concatenate([high, high, low], axis=0)).reshape(4, 256, 256)
    for b in range(8):
        table = sum(n << 2 * chip for n in range(4) for chip, to in TARGETS[n].items() if to % 4 == b // 2)
        number = (table >> 2 * z) & 3
        for t in range(4):
            out_ref[number, (b % 2) ^ core, t] = partial[t, 32 * b:32 * b + 32]


def contract(z, core, received, basis_one, basis_two):
    return pl.pallas_call(
        contract_kernel,
        in_specs=[SMEM] * 2 + [VMEM] * 3,
        out_specs=VMEM,
        out_shape=f32((4, 2, 4, 32, 256)),
        scratch_shapes=[pltpu.VMEM((4, 256, 1536), jnp.bfloat16)],
        compiler_params=params(),
        cost_estimate=pl.CostEstimate(flops=4 * 3 * 2 * 256 * 256 * 1536, bytes_accessed=6 << 20, transcendentals=0),
    )(z, core, received, basis_one.reshape(4, 2, 4, 32, 256), basis_two)


def add_kernel(a_ref, b_ref, c_ref, d_ref, own_ref, other_ref):
    for core, out_ref in enumerate((own_ref, other_ref)):
        out_ref[...] = (a_ref[core] + b_ref[core]) + (c_ref[core] + d_ref[core])


def add(received):
    return pl.pallas_call(
        add_kernel, in_specs=[VMEM] * 4, out_specs=[VMEM] * 2, out_shape=[f32((4, 32, 256))] * 2, compiler_params=params()
    )(*received)


def finish_kernel(core_ref, own_ref, swapped_ref, out_ref):
    core = core_ref[0]
    out_ref[pl.ds(4 * core, 4)] = own_ref[...]
    out_ref[pl.ds(4 - 4 * core, 4)] = swapped_ref[...]


def finish(core, own, swapped):
    return pl.pallas_call(
        finish_kernel, in_specs=[SMEM, VMEM, VMEM], out_specs=VMEM, out_shape=f32((8, 32, 256)), compiler_params=params()
    )(core, own, swapped)


def on_device(species_field, basis_one, basis_two):
    z = sum(lax.axis_index(axis) * size for axis, size in (("zh", 4), ("zp", 2), ("zn", 1))).astype(jnp.int32).reshape(1)
    core = lax.axis_index("c").astype(jnp.int32).reshape(1)
    field, z_after, core_after = lax.optimization_barrier((species_field, z, core))
    moved = lax.all_to_all(field, AXES, split_axis=0, concat_axis=0, axis_index_groups=groups(), tiled=True)
    parts = contract(z_after, core_after, moved.reshape(4, 2, 4, 2, 4, 32, 128), basis_one, basis_two)
    own, other = add([send(parts[number], number) for number in ORDER])
    return finish(core, own, lax.ppermute(other, "c", [(0, 1), (1, 0)]))


def solution(mesh):
    fine = Mesh(mesh.devices.reshape(SIZES), AXES)
    placed = (P(None, ("y", "zh", "x"), ("zp", "zn", "c")), P(), P())
    return jax.shard_map(
        on_device, mesh=fine, in_specs=placed, out_specs=P(("y", "zh", "x"), ("zp", "zn", "c"), None), check_vma=False
    )
```

```python
import functools

import jax
import jax.numpy as jnp
from jax import lax
from jax.experimental import pallas as pl
from jax.experimental.pallas import tpu as pltpu
from jax.sharding import Mesh, PartitionSpec as P

AXES = ("y", "zh", "x", "zp", "zn", "c")
SIZES = (4, 2, 4, 2, 2, 2)
FIRST = (1, 2, 4, 7)
SENDS = ((2, 1, 3, 0), (3, 0, 2, 1), (0, 3, 1, 2), (1, 2, 0, 3))
TARGETS = [dict(zip(FIRST, to)) | {7 - z: 7 - t for z, t in zip(FIRST, to)} for to in SENDS]
ORDER = (1, 2, 3, 0)
VMEM = pl.BlockSpec(memory_space=pltpu.VMEM)
SMEM = pl.BlockSpec(memory_space=pltpu.SMEM)
f32 = functools.partial(jax.ShapeDtypeStruct, dtype=jnp.float32)
dot = functools.partial(jnp.dot, preferred_element_type=jnp.float32)
params = functools.partial(pltpu.CompilerParams, vmem_limit_bytes=24 << 20)


def device(y, z, x, c):
    return (((y * 2 + z // 4) * 4 + x) * 4 + z % 4) * 2 + c


def groups():
    halves = [sorted((z, z + 1), key=lambda chip: chip not in FIRST) for z in range(0, 8, 2)]
    return [[device(y, z, x, c) for y in range(4) for z in pair for x in range(4) for c in range(2)] for pair in halves]


def send(value, number):
    pairs = []
    for y in range(4):
        for z in range(8):
            for x in range(4):
                for c in range(2):
                    pairs.append((device(y, z, x, c), device(y, TARGETS[number][z], x, c)))
    return lax.ppermute(value, AXES, pairs)


def split(value):
    high = value.astype(jnp.bfloat16)
    return high, (value - high.astype(jnp.float32)).astype(jnp.bfloat16)


def contract_kernel(z_ref, core_ref, x_ref, one_ref, two_ref, out_ref, reduced_ref):
    z, core = z_ref[0], core_ref[0]
    first = 1 - (z // 4 ^ z // 2 % 2)
    high, low = split(one_ref[:, z // 4].reshape(512, 256).T)
    one = jnp.concatenate([high, high, low], axis=1)
    for t in range(4):
        block = [x_ref[:, first ^ zn, :, c, t].reshape(512, 128) for zn in range(2) for c in range(2)]
        high, low = split(jnp.concatenate(block, axis=1))
        high, low = split(dot(one, jnp.concatenate([high, low, high], axis=0)))
        reduced_ref[t] = jnp.concatenate([high, low, high], axis=1)
    high, low = split(two_ref[pl.ds(pl.multiple_of(z // 2 % 2 * 512, 512), 512)])
    partial = dot(reduced_ref[...].reshape(1024, 1536), jnp.concatenate([high, high, low], axis=0)).reshape(4, 256, 256)
    for b in range(8):
        table = sum(n << 2 * chip for n in range(4) for chip, to in TARGETS[n].items() if to % 4 == b // 2)
        number = (table >> 2 * z) & 3
        for t in range(4):
            out_ref[number, (b % 2) ^ core, t] = partial[t, 32 * b:32 * b + 32]


def contract(z, core, received, basis_one, basis_two):
    return pl.pallas_call(
        contract_kernel,
        in_specs=[SMEM] * 2 + [VMEM] * 3,
        out_specs=VMEM,
        out_shape=f32((4, 2, 4, 32, 256)),
        scratch_shapes=[pltpu.VMEM((4, 256, 1536), jnp.bfloat16)],
        compiler_params=params(),
        cost_estimate=pl.CostEstimate(flops=4 * 3 * 2 * 256 * 256 * 1536, bytes_accessed=6 << 20, transcendentals=0),
    )(z, core, received, basis_one.reshape(4, 2, 4, 32, 256), basis_two)


def add_kernel(a_ref, b_ref, c_ref, d_ref, own_ref, other_ref):
    for core, out_ref in enumerate((own_ref, other_ref)):
        out_ref[...] = (a_ref[core] + b_ref[core]) + (c_ref[core] + d_ref[core])


def add(received):
    return pl.pallas_call(
        add_kernel, in_specs=[VMEM] * 4, out_specs=[VMEM] * 2, out_shape=[f32((4, 32, 256))] * 2, compiler_params=params()
    )(*received)


def finish_kernel(core_ref, own_ref, swapped_ref, out_ref):
    core = core_ref[0]
    out_ref[pl.ds(4 * core, 4)] = own_ref[...]
    out_ref[pl.ds(4 - 4 * core, 4)] = swapped_ref[...]


def finish(core, own, swapped):
    return pl.pallas_call(
        finish_kernel, in_specs=[SMEM, VMEM, VMEM], out_specs=VMEM, out_shape=f32((8, 32, 256)), compiler_params=params()
    )(core, own, swapped)


def on_device(species_field, basis_one, basis_two):
    z = sum(lax.axis_index(axis) * size for axis, size in (("zh", 4), ("zp", 2), ("zn", 1))).astype(jnp.int32).reshape(1)
    core = lax.axis_index("c").astype(jnp.int32).reshape(1)
    field, z_after, core_after = lax.optimization_barrier((species_field, z, core))
    moved = lax.all_to_all(field, AXES, split_axis=0, concat_axis=0, axis_index_groups=groups(), tiled=True)
    parts = contract(z_after, core_after, moved.reshape(4, 2, 4, 2, 4, 32, 128), basis_one, basis_two)
    own, other = add([send(parts[number], number) for number in ORDER])
    return finish(core, own, lax.ppermute(other, "c", [(0, 1), (1, 0)]))


def solution(mesh):
    fine = Mesh(mesh.devices.reshape(SIZES), AXES)
    placed = (P(None, ("y", "zh", "x"), ("zp", "zn", "c")), P(), P())
    return jax.shard_map(
        on_device, mesh=fine, in_specs=placed, out_specs=P(("y", "zh", "x"), ("zp", "zn", "c"), None), check_vma=False
    )
```

```python
import functools

import jax
import jax.numpy as jnp
from jax import lax
from jax.experimental import pallas as pl
from jax.experimental.pallas import tpu as pltpu
from jax.sharding import Mesh, PartitionSpec as P

AXES = ("y", "zh", "x", "zp", "zn", "c")
SIZES = (4, 2, 4, 2, 2, 2)
FIRST = (1, 2, 4, 7)
SENDS = ((2, 1, 3, 0), (3, 0, 2, 1), (0, 3, 1, 2), (1, 2, 0, 3))
TARGETS = [dict(zip(FIRST, to)) | {7 - z: 7 - t for z, t in zip(FIRST, to)} for to in SENDS]
ORDER = (1, 2, 3, 0)
VMEM = pl.BlockSpec(memory_space=pltpu.VMEM)
SMEM = pl.BlockSpec(memory_space=pltpu.SMEM)
f32 = functools.partial(jax.ShapeDtypeStruct, dtype=jnp.float32)
dot = functools.partial(jnp.dot, preferred_element_type=jnp.float32)
params = functools.partial(pltpu.CompilerParams, vmem_limit_bytes=24 << 20)


def device(y, z, x, c):
    return (((y * 2 + z // 4) * 4 + x) * 4 + z % 4) * 2 + c


def groups():
    halves = [sorted((z, z + 1), key=lambda chip: chip not in FIRST) for z in range(0, 8, 2)]
    return [[device(y, z, x, c) for y in range(4) for z in pair for x in range(4) for c in range(2)] for pair in halves]


def send(value, number):
    pairs = []
    for y in range(4):
        for z in range(8):
            for x in range(4):
                for c in range(2):
                    pairs.append((device(y, z, x, c), device(y, TARGETS[number][z], x, c)))
    return lax.ppermute(value, AXES, pairs)


def split(value):
    high = value.astype(jnp.bfloat16)
    return high, (value - high.astype(jnp.float32)).astype(jnp.bfloat16)


def contract_kernel(z_ref, core_ref, x_ref, one_ref, two_ref, out_ref, reduced_ref):
    z, core = z_ref[0], core_ref[0]
    first = 1 - (z // 4 ^ z // 2 % 2)
    high, low = split(one_ref[:, z // 4].reshape(512, 256).T)
    one_high, one = high, jnp.concatenate([high, low], axis=1)
    for t in range(4):
        block = [x_ref[:, first ^ zn, :, c, t].reshape(512, 128) for zn in range(2) for c in range(2)]
        high, low = split(jnp.concatenate(block, axis=1))
        high, low = split(dot(one, jnp.concatenate([high, high], axis=0)) + dot(one_high, low))
        reduced_ref[t] = jnp.concatenate([high, low, high], axis=1)
    high, low = split(two_ref[pl.ds(pl.multiple_of(z // 2 % 2 * 512, 512), 512)])
    partial = dot(reduced_ref[...].reshape(1024, 1536), jnp.concatenate([high, high, low], axis=0)).reshape(4, 256, 256)
    for b in range(8):
        table = sum(n << 2 * chip for n in range(4) for chip, to in TARGETS[n].items() if to % 4 == b // 2)
        number = (table >> 2 * z) & 3
        for t in range(4):
            out_ref[number, (b % 2) ^ core, t] = partial[t, 32 * b:32 * b + 32]


def contract(z, core, received, basis_one, basis_two):
    return pl.pallas_call(
        contract_kernel,
        in_specs=[SMEM] * 2 + [VMEM] * 3,
        out_specs=VMEM,
        out_shape=f32((4, 2, 4, 32, 256)),
        scratch_shapes=[pltpu.VMEM((4, 256, 1536), jnp.bfloat16)],
        compiler_params=params(),
        cost_estimate=pl.CostEstimate(flops=4 * 3 * 2 * 256 * 256 * 1536, bytes_accessed=6 << 20, transcendentals=0),
    )(z, core, received, basis_one.reshape(4, 2, 4, 32, 256), basis_two)


def add_kernel(a_ref, b_ref, c_ref, d_ref, own_ref, other_ref):
    for core, out_ref in enumerate((own_ref, other_ref)):
        out_ref[...] = (a_ref[core] + b_ref[core]) + (c_ref[core] + d_ref[core])


def add(received):
    return pl.pallas_call(
        add_kernel, in_specs=[VMEM] * 4, out_specs=[VMEM] * 2, out_shape=[f32((4, 32, 256))] * 2, compiler_params=params()
    )(*received)


def finish_kernel(core_ref, own_ref, swapped_ref, out_ref):
    core = core_ref[0]
    out_ref[pl.ds(4 * core, 4)] = own_ref[...]
    out_ref[pl.ds(4 - 4 * core, 4)] = swapped_ref[...]


def finish(core, own, swapped):
    return pl.pallas_call(
        finish_kernel, in_specs=[SMEM, VMEM, VMEM], out_specs=VMEM, out_shape=f32((8, 32, 256)), compiler_params=params()
    )(core, own, swapped)


def on_device(species_field, basis_one, basis_two):
    z = sum(lax.axis_index(axis) * size for axis, size in (("zh", 4), ("zp", 2), ("zn", 1))).astype(jnp.int32).reshape(1)
    core = lax.axis_index("c").astype(jnp.int32).reshape(1)
    field, z_after, core_after = lax.optimization_barrier((species_field, z, core))
    moved = lax.all_to_all(field, AXES, split_axis=0, concat_axis=0, axis_index_groups=groups(), tiled=True)
    parts = contract(z_after, core_after, moved.reshape(4, 2, 4, 2, 4, 32, 128), basis_one, basis_two)
    own, other = add([send(parts[number], number) for number in ORDER])
    return finish(core, own, lax.ppermute(other, "c", [(0, 1), (1, 0)]))


def solution(mesh):
    fine = Mesh(mesh.devices.reshape(SIZES), AXES)
    placed = (P(None, ("y", "zh", "x"), ("zp", "zn", "c")), P(), P())
    return jax.shard_map(
        on_device, mesh=fine, in_specs=placed, out_specs=P(("y", "zh", "x"), ("zp", "zn", "c"), None), check_vma=False
    )
```
